32 devices in a mesh: tm: 2 (over y), gx: 4 (over z), gy: 4 (over x, core).
Axes of the slice: x: 2, y: 2, z: 4, core: 2. Of those that a mesh axis runs over, the one named last changes fastest.
Arguments:
- provisional: float32 [2, 3, 3, 16, 64, 1024], P('tm', None, None, None, 'gx', 'gy'), may hold values from -1.5 to 1.5
Outputs:
- corrected: float32 [2, 3, 3, 16, 64, 1024], P('tm', None, None, None, 'gx', 'gy')
The draws below stay inside these ranges and needn't reach their ends.
All inputs are finite; a program needn't handle non-finite values.
Results may differ from the reference program's by a relative error of at most 0.00002.
Values sent between devices are 32-bit elements; how exact they have to be, the bound alone decides.
A program may use at most 64 MiB of HBM per device.

```python
import jax
import jax.numpy as jnp

NZ = 16
SLICES = 2
NX = 64
NY = 1024
N_TM = 2


def level_of(key, dims, split, low, high):
    factor_of, own = 1.0, jax.random.fold_in(key, 6)
    for position, blocks in split:
        steps = jnp.exp(jax.random.uniform(jax.random.fold_in(own, position), (blocks,), jnp.float32, low / len(split), high / len(split)))
        factor_of = factor_of * jnp.repeat(steps, dims[position] // blocks).reshape([-1 if axis == position else 1 for axis in range(len(dims))])
    return factor_of


def noise(rng, dims, scale, reach, split=(), kind=jnp.bfloat16):
    drawn = jax.random.normal(rng, dims, jnp.float32) * scale
    if len(split) > 0:
        drawn = level_of(rng, dims, split, -0.22, 0.18) * drawn
    return jnp.clip(drawn, min=-reach, max=reach).astype(kind)


def setup_inputs(seed: int = 0) -> dict:
    splits = jax.random.split(jax.random.key(seed), 2)
    return {
        "provisional": noise(splits[0], (SLICES, 3, 3, NZ, NX, NY), 0.25, 1.5, ((0, 2), (4, 4), (5, 4)), jnp.float32),
    }


viscosity = 0.1
slice_step = 0.25
half_step = 0.125
first_row = (5.0 / 24.0, 1.0 / 3.0, -1.0 / 24.0)
second_row = (-1.0 / 24.0, 1.0 / 3.0, 5.0 / 24.0)


def tendency(padded, spacing):
    centre = padded[:, :, 1:-1, 1:-1]
    east_side = padded[:, :, 2:, 1:-1]
    west_side = padded[:, :, :-2, 1:-1]
    north_side = padded[:, :, 1:-1, 2:]
    south_side = padded[:, :, 1:-1, :-2]
    upper_side = jnp.roll(centre, -1, axis=1)
    lower_side = jnp.roll(centre, 1, axis=1)
    change_first = 0.5 * (east_side - west_side)
    change_second = (0.5 / spacing) * (north_side - south_side)
    change_third = 0.5 * (upper_side - lower_side)
    laplace = (east_side + west_side - 2.0 * centre) + (north_side + south_side - 2.0 * centre) / (spacing * spacing) + (upper_side + lower_side - 2.0 * centre)
    transport = centre[0:1] * change_first + centre[1:2] * change_second + centre[2:3] * change_third
    return viscosity * laplace - transport


def evaluate(field, spacing):
    return tendency(jnp.pad(field, ((0, 0), (0, 0), (1, 1), (1, 1))), spacing)


def quadrature(values, weights):
    return slice_step * (weights[0] * values[0] + weights[1] * values[1] + weights[2] * values[2])


def restrict(field):
    return 0.5 * (field[..., 0::2] + field[..., 1::2])


def prolong(field):
    return jnp.repeat(field, 2, axis=-1)


def reference(provisional):
    outputs = []
    carried_coarse = None
    carried_fine = None
    for slice_index in range(N_TM):
        start_node = provisional[slice_index, 0]
        middle_node = provisional[slice_index, 1]
        final_node = provisional[slice_index, 2]
        old_fluxes = (evaluate(start_node, 1.0), evaluate(middle_node, 1.0), evaluate(final_node, 1.0))
        new_middle = start_node + quadrature(old_fluxes, first_row)
        slope_middle = evaluate(new_middle, 1.0)
        new_final = new_middle + half_step * (slope_middle - old_fluxes[1]) + quadrature(old_fluxes, second_row)
        slope_final = evaluate(new_final, 1.0)
        coarse_start = restrict(start_node)
        coarse_middle = restrict(new_middle)
        coarse_final = restrict(new_final)
        new_fluxes = (old_fluxes[0], slope_middle, slope_final)
        integral_first = restrict(quadrature(new_fluxes, first_row))
        integral_second = restrict(quadrature(new_fluxes, second_row))
        base_start = evaluate(coarse_start, 2.0)
        base_middle = evaluate(coarse_middle, 2.0)
        chain_start = coarse_start if slice_index == 0 else carried_coarse
        chain_middle = chain_start + half_step * (evaluate(chain_start, 2.0) - base_start) + integral_first
        chain_final = chain_middle + half_step * (evaluate(chain_middle, 2.0) - base_middle) + integral_second
        out_middle = new_middle + prolong(chain_middle - coarse_middle)
        out_final = new_final + prolong(chain_final - coarse_final)
        out_start = start_node if slice_index == 0 else carried_fine
        outputs.append(jnp.stack([out_start, out_middle, out_final]))
        carried_coarse = chain_final
        carried_fine = out_final
    return jnp.stack(outputs)
```

```python
import functools

import jax
import jax.numpy as jnp
from jax import lax
from jax.experimental import pallas as pl
from jax.experimental.pallas import tpu as pltpu
from jax.sharding import PartitionSpec as P

viscosity = 0.1
slice_step = 0.25
half_step = 0.125
first_row = (5.0 / 24.0, 1.0 / 3.0, -1.0 / 24.0)
second_row = (-1.0 / 24.0, 1.0 / 3.0, 5.0 / 24.0)
q1 = tuple(slice_step * w for w in first_row)
q2 = tuple(slice_step * w for w in second_row)
LANES = 128


def kernel(
    n_tm, n_gx, n_gy, in_ref, out_ref,
    up, v1p, v2p, c0p, c1p, w0p, w1p, f0, s2, qa, qb, m1, m2,
    eu_s, eu_r, ev1_s, ev1_r, ev2_s, ev2_r, ew0_s, ew0_r, ew1_s, ew1_r,
    d_s, d_r, w_s, w_r,
    load_sem, send_sem, recv_sem, tm_send, tm_recv,
):
    _, _, X, Z, Y = in_ref.shape
    H = X // 2
    t, gx, gy = lax.axis_index("tm"), lax.axis_index("gx"), lax.axis_index("gy")
    has = {
        ("gx", 1): gx < n_gx - 1, ("gx", -1): gx > 0,
        ("gy", 1): gy < n_gy - 1, ("gy", -1): gy > 0,
        ("tm", 1): t < n_tm - 1, ("tm", -1): t > 0,
    }
    place = {"gx": gx, "gy": gy, "tm": t}

    def target(axis, step):
        size = {"gx": n_gx, "gy": n_gy, "tm": n_tm}[axis]
        moved = dict(place)
        moved[axis] = lax.rem(place[axis] + step + size, size)
        return (moved["tm"], moved["gx"], moved["gy"])

    load = pltpu.make_async_copy(in_ref, up.at[:, :, pl.ds(1, X)], load_sem)
    load.start()

    barrier = pltpu.get_barrier_semaphore()
    for (axis, step), there in has.items():
        @pl.when(there)
        def _(axis=axis, step=step):
            pl.semaphore_signal(
                barrier, inc=1, device_id=target(axis, step),
                device_id_type=pl.DeviceIdType.MESH,
            )
    peers = sum(jnp.where(there, 1, 0) for there in has.values())
    pl.semaphore_wait(barrier, peers)

    lane = lax.broadcasted_iota(jnp.int32, (Z, Y), 1)
    even = lane % 2 == 0
    elane = lax.broadcasted_iota(jnp.int32, (Z, LANES), 1)
    epair = elane // 2

    def remote(src, dst, p, d, axis, step):
        return pltpu.make_async_remote_copy(
            src_ref=src, dst_ref=dst, send_sem=send_sem.at[p, d], recv_sem=recv_sem.at[p, d],
            device_id=target(axis, step), device_id_type=pl.DeviceIdType.MESH,
        )

    def row(ref, i):
        return ref.at[:, :, pl.ds(i, 1)] if len(ref.shape) == 5 else ref.at[:, pl.ds(i, 1)]

    def rows_of(p, src, first, last, dst):
        return [
            (("gx", 1), remote(row(src, last), row(dst, 0), p, 0, "gx", 1)),
            (("gx", -1), remote(row(src, first), row(dst, X + 1), p, 1, "gx", -1)),
        ]

    def columns_of(p, es, er):
        return [
            (("gy", 1), remote(es.at[1], er.at[0], p, 2, "gy", 1)),
            (("gy", -1), remote(es.at[0], er.at[1], p, 3, "gy", -1)),
        ]

    def start(copies):
        for key, copy in copies:
            pl.when(has[key])(copy.start)

    def arrive(copies):
        for (axis, step), copy in copies:
            pl.when(has[(axis, -step)])(copy.wait_recv)

    def sent(copies):
        for key, copy in copies:
            pl.when(has[key])(copy.wait_send)

    def no_rows(dst):
        for key, i in ((("gx", -1), 0), (("gx", 1), X + 1)):
            @pl.when(jnp.logical_not(has[key]))
            def _(i=i):
                where_ = row(dst, i)
                where_[...] = jnp.zeros(where_.shape, jnp.float32)

    def no_columns(er):
        for key, i in ((("gy", -1), 0), (("gy", 1), 1)):
            @pl.when(jnp.logical_not(has[key]))
            def _(i=i):
                er[i] = jnp.zeros(er.shape[1:], jnp.float32)

    def G(get, x, low, high, k):
        mid = [get(c, x + 1) for c in range(3)]
        a = [0.5 * mid[0], (0.5 / k) * mid[1], 0.5 * mid[2]]
        nu = [viscosity, viscosity / (k * k), viscosity]
        ahead = [nu[i] - a[i] for i in range(3)]
        behind = [nu[i] + a[i] for i in range(3)]
        result = []
        for c in range(3):
            u = mid[c]
            at = c * X + x
            if k == 1:
                h = pltpu.roll(high, LANES - 1 - at, 1)
                l = pltpu.roll(low, lax.rem(LANES - at, LANES), 1)
            else:
                h = pltpu.roll(high, LANES - 2 - 2 * at, 1)
                l = pltpu.roll(low, lax.rem(LANES - 2 * at, LANES), 1)
            wide = Y // LANES
            north = jnp.where(lane >= Y - k, jnp.concatenate([h] * wide, 1), pltpu.roll(u, Y - k, 1))
            south = jnp.where(lane < k, jnp.concatenate([l] * wide, 1), pltpu.roll(u, k, 1))
            result.append(
                (ahead[0] * get(c, x + 2) + behind[0] * get(c, x))
                + (ahead[1] * north + behind[1] * south)
                + (ahead[2] * pltpu.roll(u, Z - 1, 0) + behind[2] * pltpu.roll(u, 1, 0))
                - (2.0 * sum(nu)) * u
            )
        return result

    def R(u):
        return 0.5 * (u + jnp.where(even, pltpu.roll(u, Y - 1, 1), pltpu.roll(u, 1, 1)))

    def put(acc, column, at, k):
        return jnp.where((elane if k == 1 else epair) == at, column, acc)

    def put_both(pair, u, at, k):
        return (put(pair[0], u[:, :1], at, k), put(pair[1], u[:, Y - 1:], at, k))

    blank = jnp.zeros((Z, LANES), jnp.float32)
    blanks = (blank, blank)

    def loop(body, carry, count=X):
        return lax.fori_loop(0, count, body, carry)

    u_rows = rows_of(0, in_ref, 0, X - 1, up)
    start(u_rows)
    no_rows(up)
    no_columns(eu_r)
    load.wait()

    def pack_u(x, carry):
        nodes, coarse = list(carry[:3]), carry[3]
        for c in range(3):
            at = c * X + x
            for n in range(3):
                nodes[n] = put_both(nodes[n], up[n, c, x + 1], at, 1)
            coarse = put_both(coarse, R(up[0, c, x + 1]), at, 2)
        return (*nodes, coarse)

    packed = loop(pack_u, (blanks,) * 4)
    for n in range(4):
        for side in range(2):
            eu_s[side, n] = packed[n][side]
    u_columns = columns_of(0, eu_s, eu_r)
    start(u_columns)
    arrive(u_rows)
    arrive(u_columns)

    def sweep_first(x, carry):
        fine, coarse = carry
        fluxes = [
            G(lambda c, i, n=n: up[n, c, i], x, eu_r[0, n], eu_r[1, n], 1) for n in range(3)
        ]
        for c in range(3):
            a, b, d = (fluxes[n][c] for n in range(3))
            v1 = up[0, c, x + 1] + (q1[0] * a + q1[1] * b + q1[2] * d)
            v1p[c, x + 1] = v1
            f0[c, x] = a
            s2[c, x] = q2[0] * a + (q2[1] - half_step) * b + q2[2] * d
            at = c * X + x
            fine = put_both(fine, v1, at, 1)
            coarse = put_both(coarse, R(v1), at, 2)
        return fine, coarse

    fine, coarse = loop(sweep_first, (blanks, blanks))
    for side in range(2):
        ev1_s[side, 0] = fine[side]
        ev1_s[side, 1] = coarse[side]
    v1_copies = rows_of(1, v1p, 1, X, v1p) + columns_of(1, ev1_s, ev1_r)
    start(v1_copies)
    no_rows(v1p)
    no_columns(ev1_r)

    def restrict_start(i, _):
        for c in range(3):
            c0p[c, i] = R(up[0, c, i])
        return 0

    loop(restrict_start, 0, X + 2)

    @pl.when(has[("tm", -1)])
    def _():
        def base_start(x, _):
            b0 = G(lambda c, i: c0p[c, i], x, eu_r[0, 3], eu_r[1, 3], 2)
            for c in range(3):
                m1[c, x] = -half_step * b0[c]
            return 0

        loop(base_start, 0)

    arrive(v1_copies)

    def sweep_second(x, fine):
        h1 = G(lambda c, i: v1p[c, i], x, ev1_r[0, 0], ev1_r[1, 0], 1)
        for c in range(3):
            v2 = v1p[c, x + 1] + half_step * h1[c] + s2[c, x]
            v2p[c, x + 1] = v2
            a = f0[c, x]
            qa[c, x] = q1[0] * a + q1[1] * h1[c]
            qb[c, x] = q2[0] * a + q2[1] * h1[c]
            fine = put_both(fine, v2, c * X + x, 1)
        return fine

    fine = loop(sweep_second, blanks)
    for side in range(2):
        ev2_s[side, 0] = fine[side]
    v2_copies = rows_of(2, v2p, 1, X, v2p) + columns_of(2, ev2_s, ev2_r)
    start(v2_copies)
    no_rows(v2p)
    no_columns(ev2_r)

    def detail(x, _):
        for c in range(3):
            a, b = v2p[c, x + 1], v2p[c, x + H + 1]
            d_s[c, x] = jnp.where(even, a - R(a), b - R(b))
        return 0

    def along(src, dst, p):
        return pltpu.make_async_remote_copy(
            src_ref=src, dst_ref=dst, send_sem=tm_send.at[p], recv_sem=tm_recv.at[p],
            device_id=target("tm", 1), device_id_type=pl.DeviceIdType.MESH,
        )

    d_copy = [(("tm", 1), along(d_s, d_r, 0))]
    w_copy = [(("tm", 1), along(w_s, w_r, 1))]

    @pl.when(has[("tm", 1)])
    def _():
        loop(detail, 0, H)

    start(d_copy)

    def restrict_middle(i, _):
        for c in range(3):
            c1p[c, i] = R(v1p[c, i])
        return 0

    loop(restrict_middle, 0, X + 2)

    def base_middle(x, _):
        b1 = G(lambda c, i: c1p[c, i], x, ev1_r[0, 1], ev1_r[1, 1], 2)
        for c in range(3):
            m2[c, x] = -half_step * b1[c]
        return 0

    loop(base_middle, 0)
    arrive(v2_copies)

    leader = t == 0

    def sweep_third(x, coarse):
        h2 = G(lambda c, i: v2p[c, i], x, ev2_r[0, 0], ev2_r[1, 0], 1)
        for c in range(3):
            a1 = R(qa[c, x] + q1[2] * h2[c])
            a2 = R(qb[c, x] + q2[2] * h2[c])
            m2[c, x] = m2[c, x] + a2
            w1 = c0p[c, x + 1] + a1
            w1p[c, x + 1] = w1
            qa[c, x] = a1
            coarse = put_both(coarse, w1, c * X + x, 2)
        return coarse

    coarse = loop(sweep_third, blanks)

    w0_copies = rows_of(3, w0p, 1, X, w0p) + columns_of(3, ew0_s, ew0_r)
    w1_copies = rows_of(4, w1p, 1, X, w1p) + columns_of(4, ew1_s, ew1_r)

    @pl.when(leader)
    def _():
        for side in range(2):
            ew1_s[side, 0] = coarse[side]

    @pl.when(has[("tm", -1)])
    def _():
        arrive(w_copy)

        def unpack(x, coarse):
            for c in range(3):
                w = w_r[c, x]
                a = jnp.where(even, w, pltpu.roll(w, 1, 1))
                b = jnp.where(even, pltpu.roll(w, Y - 1, 1), w)
                w0p[c, x + 1] = a
                w0p[c, x + H + 1] = b
                coarse = put_both(coarse, a, c * X + x, 2)
                coarse = put_both(coarse, b, c * X + x + H, 2)
            return coarse

        coarse = loop(unpack, blanks, H)
        for side in range(2):
            ew0_s[side, 0] = coarse[side]
        start(w0_copies)
        no_rows(w0p)
        no_columns(ew0_r)
        arrive(w0_copies)

        def chain_middle(x, coarse):
            g = G(lambda c, i: w0p[c, i], x, ew0_r[0, 0], ew0_r[1, 0], 2)
            for c in range(3):
                w1 = w0p[c, x + 1] + half_step * g[c] + (m1[c, x] + qa[c, x])
                w1p[c, x + 1] = w1
                coarse = put_both(coarse, w1, c * X + x, 2)
            return coarse

        coarse = loop(chain_middle, blanks)
        for side in range(2):
            ew1_s[side, 0] = coarse[side]

    start(w1_copies)
    no_rows(w1p)
    no_columns(ew1_r)

    def middle_out(x, _):
        for c in range(3):
            out_ref[1, c, x] = v1p[c, x + 1] + (w1p[c, x + 1] - c1p[c, x + 1])
        return 0

    loop(middle_out, 0)

    @pl.when(leader)
    def _():
        def start_out(x, _):
            for c in range(3):
                out_ref[0, c, x] = up[0, c, x + 1]
            return 0

        loop(start_out, 0)

    arrive(w1_copies)

    def chain_final(x, _):
        low, high = ew1_r[0, 0], ew1_r[1, 0]
        ga = G(lambda c, i: w1p[c, i], x, low, high, 2)
        gb = G(lambda c, i: w1p[c, i], x + H, low, high, 2)
        for c in range(3):
            ends = []
            for g, i in ((ga, x), (gb, x + H)):
                w2 = w1p[c, i + 1] + half_step * g[c] + m2[c, i]
                v2 = v2p[c, i + 1]
                out_ref[2, c, i] = v2 + (w2 - R(v2))
                ends.append(w2)
            w_s[c, x] = jnp.where(even, ends[0], ends[1])
        return 0

    loop(chain_final, 0, H)
    start(w_copy)

    @pl.when(has[("tm", -1)])
    def _():
        arrive(d_copy)

        def start_out(x, _):
            for c in range(3):
                d = d_r[c, x]
                a = jnp.where(even, d, -pltpu.roll(d, 1, 1))
                b = jnp.where(even, -pltpu.roll(d, Y - 1, 1), d)
                out_ref[0, c, x] = w0p[c, x + 1] + a
                out_ref[0, c, x + H] = w0p[c, x + H + 1] + b
            return 0

        loop(start_out, 0, H)
        sent(w0_copies)

    for copies in (u_rows, u_columns, v1_copies, v2_copies, w1_copies, d_copy, w_copy):
        sent(copies)


def per_device(sizes, provisional):
    block = jnp.swapaxes(provisional[0], 2, 3)
    _, _, X, Z, Y = block.shape
    f32 = jnp.float32
    padded = pltpu.VMEM((3, X + 2, Z, Y), f32)
    plain = pltpu.VMEM((3, X, Z, Y), f32)
    half = pltpu.VMEM((3, X // 2, Z, Y), f32)

    def edges(count):
        return [pltpu.VMEM((2, count, Z, LANES), f32)] * 2

    out = pl.pallas_call(
        functools.partial(kernel, *sizes),
        out_shape=jax.ShapeDtypeStruct(block.shape, f32),
        in_specs=[pl.BlockSpec(memory_space=pl.ANY)],
        out_specs=pl.BlockSpec(memory_space=pltpu.VMEM),
        scratch_shapes=[
            pltpu.VMEM((3, 3, X + 2, Z, Y), f32),
            *[padded] * 6,
            *[plain] * 6,
            *edges(4), *edges(2), *edges(1), *edges(1), *edges(1),
            *[half] * 4,
            pltpu.SemaphoreType.DMA,
            pltpu.SemaphoreType.DMA((5, 4)),
            pltpu.SemaphoreType.DMA((5, 4)),
            pltpu.SemaphoreType.DMA((2,)),
            pltpu.SemaphoreType.DMA((2,)),
        ],
        compiler_params=pltpu.CompilerParams(
            collective_id=0, has_side_effects=True, vmem_limit_bytes=40 * 1024 * 1024
        ),
    )(block)
    return jnp.swapaxes(out, 2, 3)[None]


def solution(mesh):
    sizes = tuple(mesh.shape[axis] for axis in ("tm", "gx", "gy"))
    spec = P("tm", None, None, None, "gx", "gy")
    return jax.shard_map(
        functools.partial(per_device, sizes), mesh=mesh, in_specs=(spec,), out_specs=spec,
        check_vma=False,
    )
```

```python
import functools

import jax
import jax.numpy as jnp
from jax import lax
from jax.experimental import pallas as pl
from jax.experimental.pallas import tpu as pltpu
from jax.sharding import PartitionSpec as P

viscosity = 0.1
slice_step = 0.25
half_step = 0.125
first_row = (5.0 / 24.0, 1.0 / 3.0, -1.0 / 24.0)
second_row = (-1.0 / 24.0, 1.0 / 3.0, 5.0 / 24.0)
q1 = tuple(slice_step * w for w in first_row)
q2 = tuple(slice_step * w for w in second_row)
LANES = 128


def kernel(
    n_tm, n_gx, n_gy, in_ref, out_ref,
    up, v1p, v2p, c0p, c1p, w0p, w1p, w2p, f0, s2, qa, qb, m1, m2,
    eu_s, eu_r, ev1_s, ev1_r, ev2_s, ev2_r, ew0_s, ew0_r, ew1_s, ew1_r,
    d_s, d_r, w_s, w_r,
    load_sem, send_sem, recv_sem, tm_send, tm_recv,
):
    _, _, X, Z, Y = in_ref.shape
    H = X // 2
    t, gx, gy = lax.axis_index("tm"), lax.axis_index("gx"), lax.axis_index("gy")
    has = {
        ("gx", 1): gx < n_gx - 1, ("gx", -1): gx > 0,
        ("gy", 1): gy < n_gy - 1, ("gy", -1): gy > 0,
        ("tm", 1): t < n_tm - 1, ("tm", -1): t > 0,
    }
    for axis in ("gx", "gy"):
        for step in (1, -1):
            for slice_ in (1, -1):
                has[(axis, step, slice_)] = jnp.logical_and(has[(axis, step)], has[("tm", slice_)])
    place = {"gx": gx, "gy": gy, "tm": t}

    def target(axis, step, slice_=0):
        size = {"gx": n_gx, "gy": n_gy, "tm": n_tm}
        moved = dict(place)
        moved[axis] = lax.rem(place[axis] + step + size[axis], size[axis])
        if slice_ != 0:
            moved["tm"] = lax.rem(t + slice_ + n_tm, n_tm)
        return (moved["tm"], moved["gx"], moved["gy"])

    load = pltpu.make_async_copy(in_ref, up.at[:, :, pl.ds(1, X)], load_sem)
    load.start()

    barrier = pltpu.get_barrier_semaphore()
    for peer, there in has.items():
        @pl.when(there)
        def _(peer=peer):
            pl.semaphore_signal(
                barrier, inc=1, device_id=target(*peer),
                device_id_type=pl.DeviceIdType.MESH,
            )
    peers = sum(jnp.where(there, 1, 0) for there in has.values())
    pl.semaphore_wait(barrier, peers)

    lane = lax.broadcasted_iota(jnp.int32, (Z, Y), 1)
    even = lane % 2 == 0
    elane = lax.broadcasted_iota(jnp.int32, (Z, LANES), 1)
    epair = elane // 2

    def remote(src, dst, p, d, axis, step, slice_=0):
        return pltpu.make_async_remote_copy(
            src_ref=src, dst_ref=dst, send_sem=send_sem.at[p, d], recv_sem=recv_sem.at[p, d],
            device_id=target(axis, step, slice_), device_id_type=pl.DeviceIdType.MESH,
        )

    def row(ref, i):
        return ref.at[:, :, pl.ds(i, 1)] if len(ref.shape) == 5 else ref.at[:, pl.ds(i, 1)]

    def rows_of(p, src, first, last, dst):
        return [
            (("gx", 1), remote(row(src, last), row(dst, 0), p, 0, "gx", 1)),
            (("gx", -1), remote(row(src, first), row(dst, X + 1), p, 1, "gx", -1)),
        ]

    def columns_of(p, es, er):
        return [
            (("gy", 1), remote(es.at[1], er.at[0], p, 2, "gy", 1)),
            (("gy", -1), remote(es.at[0], er.at[1], p, 3, "gy", -1)),
        ]

    def start(copies):
        for key, copy in copies:
            pl.when(has[key])(copy.start)

    def arrive(copies):
        for (axis, *steps), copy in copies:
            pl.when(has[(axis, *[-step for step in steps])])(copy.wait_recv)

    def sent(copies):
        for key, copy in copies:
            pl.when(has[key])(copy.wait_send)

    def no_rows(dst):
        for key, i in ((("gx", -1), 0), (("gx", 1), X + 1)):
            @pl.when(jnp.logical_not(has[key]))
            def _(i=i):
                where_ = row(dst, i)
                where_[...] = jnp.zeros(where_.shape, jnp.float32)

    def no_columns(er):
        for key, i in ((("gy", -1), 0), (("gy", 1), 1)):
            @pl.when(jnp.logical_not(has[key]))
            def _(i=i):
                er[i] = jnp.zeros(er.shape[1:], jnp.float32)

    def G(get, x, low, high, k):
        mid = [get(c, x + 1) for c in range(3)]
        a = [0.5 * mid[0], (0.5 / k) * mid[1], 0.5 * mid[2]]
        nu = [viscosity, viscosity / (k * k), viscosity]
        ahead = [nu[i] - a[i] for i in range(3)]
        behind = [nu[i] + a[i] for i in range(3)]
        result = []
        for c in range(3):
            u = mid[c]
            at = c * X + x
            if k == 1:
                h = pltpu.roll(high, LANES - 1 - at, 1)
                l = pltpu.roll(low, lax.rem(LANES - at, LANES), 1)
            else:
                h = pltpu.roll(high, LANES - 2 - 2 * at, 1)
                l = pltpu.roll(low, lax.rem(LANES - 2 * at, LANES), 1)
            wide = Y // LANES
            north = jnp.where(lane >= Y - k, jnp.concatenate([h] * wide, 1), pltpu.roll(u, Y - k, 1))
            south = jnp.where(lane < k, jnp.concatenate([l] * wide, 1), pltpu.roll(u, k, 1))
            result.append(
                (ahead[0] * get(c, x + 2) + behind[0] * get(c, x))
                + (ahead[1] * north + behind[1] * south)
                + (ahead[2] * pltpu.roll(u, Z - 1, 0) + behind[2] * pltpu.roll(u, 1, 0))
                - (2.0 * sum(nu)) * u
            )
        return result

    def R(u):
        return 0.5 * (u + jnp.where(even, pltpu.roll(u, Y - 1, 1), pltpu.roll(u, 1, 1)))

    def put(acc, column, at, k):
        return jnp.where((elane if k == 1 else epair) == at, column, acc)

    def put_both(pair, u, at, k):
        return (put(pair[0], u[:, :1], at, k), put(pair[1], u[:, Y - 1:], at, k))

    blank = jnp.zeros((Z, LANES), jnp.float32)
    blanks = (blank, blank)

    def loop(body, carry, count=X, first=0):
        return lax.fori_loop(first, count, body, carry)

    def edges_first(body, carry, copies):
        carry = loop(lambda i, carry: body(i * (X - 1), carry), carry, 2)
        start(copies)
        return loop(body, carry, X - 1, 1)

    u_rows = rows_of(0, in_ref, 0, X - 1, up)
    start(u_rows)
    no_rows(up)
    no_columns(eu_r)
    load.wait()

    def pack_u(x, carry):
        nodes, coarse = list(carry[:3]), carry[3]
        for c in range(3):
            at = c * X + x
            for n in range(3):
                nodes[n] = put_both(nodes[n], up[n, c, x + 1], at, 1)
            coarse = put_both(coarse, R(up[0, c, x + 1]), at, 2)
        return (*nodes, coarse)

    packed = loop(pack_u, (blanks,) * 4)
    for n in range(4):
        for side in range(2):
            eu_s[side, n] = packed[n][side]
    u_columns = columns_of(0, eu_s, eu_r)
    start(u_columns)
    arrive(u_rows)
    arrive(u_columns)

    def sweep_first(x, carry):
        fine, coarse = carry
        fluxes = [
            G(lambda c, i, n=n: up[n, c, i], x, eu_r[0, n], eu_r[1, n], 1) for n in range(3)
        ]
        for c in range(3):
            a, b, d = (fluxes[n][c] for n in range(3))
            v1 = up[0, c, x + 1] + (q1[0] * a + q1[1] * b + q1[2] * d)
            v1p[c, x + 1] = v1
            f0[c, x] = a
            s2[c, x] = q2[0] * a + (q2[1] - half_step) * b + q2[2] * d
            at = c * X + x
            fine = put_both(fine, v1, at, 1)
            coarse = put_both(coarse, R(v1), at, 2)
        return fine, coarse

    v1_rows = rows_of(1, v1p, 1, X, v1p)
    v1_columns = columns_of(1, ev1_s, ev1_r)
    v1_copies = v1_rows + v1_columns
    fine, coarse = edges_first(sweep_first, (blanks, blanks), v1_rows)
    for side in range(2):
        ev1_s[side, 0] = fine[side]
        ev1_s[side, 1] = coarse[side]
    start(v1_columns)
    no_rows(v1p)
    no_columns(ev1_r)

    def restrict_start(i, _):
        for c in range(3):
            c0p[c, i] = R(up[0, c, i])
        return 0

    loop(restrict_start, 0, X + 2)

    @pl.when(has[("tm", -1)])
    def _():
        def base_start(x, _):
            b0 = G(lambda c, i: c0p[c, i], x, eu_r[0, 3], eu_r[1, 3], 2)
            for c in range(3):
                m1[c, x] = -half_step * b0[c]
            return 0

        loop(base_start, 0)

    arrive(v1_copies)

    def sweep_second(x, fine):
        h1 = G(lambda c, i: v1p[c, i], x, ev1_r[0, 0], ev1_r[1, 0], 1)
        for c in range(3):
            v2 = v1p[c, x + 1] + half_step * h1[c] + s2[c, x]
            v2p[c, x + 1] = v2
            a = f0[c, x]
            qa[c, x] = q1[0] * a + q1[1] * h1[c]
            qb[c, x] = q2[0] * a + q2[1] * h1[c]
            fine = put_both(fine, v2, c * X + x, 1)
        return fine

    v2_rows = rows_of(2, v2p, 1, X, v2p)
    v2_columns = columns_of(2, ev2_s, ev2_r)
    v2_copies = v2_rows + v2_columns
    fine = edges_first(sweep_second, blanks, v2_rows)
    for side in range(2):
        ev2_s[side, 0] = fine[side]
    start(v2_columns)
    no_rows(v2p)
    no_columns(ev2_r)

    def detail(x, _):
        for c in range(3):
            a, b = v2p[c, x + 1], v2p[c, x + H + 1]
            d_s[c, x] = jnp.where(even, a - R(a), b - R(b))
        return 0

    def along(src, dst, p):
        return pltpu.make_async_remote_copy(
            src_ref=src, dst_ref=dst, send_sem=tm_send.at[p], recv_sem=tm_recv.at[p],
            device_id=target("tm", 1), device_id_type=pl.DeviceIdType.MESH,
        )

    d_copy = [(("tm", 1), along(d_s, d_r, 0))]
    spans = [(0, 1), (H - 1, 1)]
    spans += [(i, min(2, H - 1 - i)) for i in range(1, H - 1, 2)]
    spans = spans[: max(1, H)]
    w_parts = [
        [(("tm", 1), along(w_s.at[:, pl.ds(i, n)], w_r.at[:, pl.ds(i, n)], 1 + j))]
        for j, (i, n) in enumerate(spans)
    ]
    w0_rows = [
        (("gx", 1, 1), remote(row(w2p, X - 1), row(w0p, 0), 3, 0, "gx", 1, 1)),
        (("gx", -1, 1), remote(row(w2p, 0), row(w0p, X + 1), 3, 1, "gx", -1, 1)),
    ]
    w0_columns = [
        (("gy", 1, 1), remote(ew0_s.at[1], ew0_r.at[0], 3, 2, "gy", 1, 1)),
        (("gy", -1, 1), remote(ew0_s.at[0], ew0_r.at[1], 3, 3, "gy", -1, 1)),
    ]

    @pl.when(has[("tm", 1)])
    def _():
        loop(detail, 0, H)

    start(d_copy)

    def restrict_middle(i, _):
        for c in range(3):
            c1p[c, i] = R(v1p[c, i])
        return 0

    loop(restrict_middle, 0, X + 2)

    def base_middle(x, _):
        b1 = G(lambda c, i: c1p[c, i], x, ev1_r[0, 1], ev1_r[1, 1], 2)
        for c in range(3):
            m2[c, x] = -half_step * b1[c]
        return 0

    loop(base_middle, 0)
    arrive(v2_copies)

    leader = t == 0

    def sweep_third(x, coarse):
        h2 = G(lambda c, i: v2p[c, i], x, ev2_r[0, 0], ev2_r[1, 0], 1)
        for c in range(3):
            a1 = R(qa[c, x] + q1[2] * h2[c])
            a2 = R(qb[c, x] + q2[2] * h2[c])
            m2[c, x] = m2[c, x] + a2
            if coarse is None:
                m1[c, x] = m1[c, x] + a1
            else:
                w1 = c0p[c, x + 1] + a1
                w1p[c, x + 1] = w1
                coarse = put_both(coarse, w1, c * X + x, 2)
        return coarse

    w1_rows = rows_of(4, w1p, 1, X, w1p)
    w1_columns = columns_of(4, ew1_s, ew1_r)
    w1_copies = w1_rows + w1_columns

    @pl.when(leader)
    def _():
        coarse = edges_first(sweep_third, blanks, w1_rows)
        for side in range(2):
            ew1_s[side, 0] = coarse[side]

    @pl.when(has[("tm", -1)])
    def _():
        loop(lambda x, _: sweep_third(x, None) or 0, 0)
        no_rows(w0p)
        no_columns(ew0_r)

        def unpack(x, _):
            for c in range(3):
                w = w_r[c, x]
                w0p[c, x + 1] = jnp.where(even, w, pltpu.roll(w, 1, 1))
                w0p[c, x + H + 1] = jnp.where(even, pltpu.roll(w, Y - 1, 1), w)
            return 0

        for part, (i, n) in zip(w_parts, spans):
            arrive(part)
            loop(unpack, 0, i + n, i)
        arrive(w0_rows)
        arrive(w0_columns)

        def chain_middle(x, coarse):
            g = G(lambda c, i: w0p[c, i], x, ew0_r[0, 0], ew0_r[1, 0], 2)
            for c in range(3):
                w1 = w0p[c, x + 1] + half_step * g[c] + m1[c, x]
                w1p[c, x + 1] = w1
                coarse = put_both(coarse, w1, c * X + x, 2)
            return coarse

        coarse = edges_first(chain_middle, blanks, w1_rows)
        for side in range(2):
            ew1_s[side, 0] = coarse[side]

    start(w1_columns)
    no_rows(w1p)
    no_columns(ew1_r)

    def middle_out(x, _):
        for c in range(3):
            out_ref[1, c, x] = v1p[c, x + 1] + (w1p[c, x + 1] - c1p[c, x + 1])
        return 0

    loop(middle_out, 0)

    @pl.when(leader)
    def _():
        def start_out(x, _):
            for c in range(3):
                out_ref[0, c, x] = up[0, c, x + 1]
            return 0

        loop(start_out, 0)

    @pl.when(has[("tm", -1)])
    def _():
        arrive(d_copy)

        def start_out(x, _):
            for c in range(3):
                d = d_r[c, x]
                a = jnp.where(even, d, -pltpu.roll(d, 1, 1))
                b = jnp.where(even, -pltpu.roll(d, Y - 1, 1), d)
                out_ref[0, c, x] = w0p[c, x + 1] + a
                out_ref[0, c, x + H] = w0p[c, x + H + 1] + b
            return 0

        loop(start_out, 0, H)

    arrive(w1_copies)

    def chain_end(x):
        g = G(lambda c, i: w1p[c, i], x, ew1_r[0, 0], ew1_r[1, 0], 2)
        return [w1p[c, x + 1] + half_step * g[c] + m2[c, x] for c in range(3)]

    def end_out(c, x, w2):
        v2 = v2p[c, x + 1]
        out_ref[2, c, x] = v2 + (w2 - R(v2))

    @pl.when(has[("tm", 1)])
    def _():
        def pair(x, coarse):
            ends = (chain_end(x), chain_end(x + H))
            for c in range(3):
                w_s[c, x] = jnp.where(even, ends[0][c], ends[1][c])
                for end, i in zip(ends, (x, x + H)):
                    w2p[c, i] = end[c]
                    coarse = put_both(coarse, end[c], c * X + i, 2)
            return coarse

        coarse = blanks
        for j, (part, (i, n)) in enumerate(zip(w_parts, spans)):
            coarse = loop(pair, coarse, i + n, i)
            start(part)
            if j == min(1, len(spans) - 1):
                start(w0_rows)
        for side in range(2):
            ew0_s[side, 0] = coarse[side]
        start(w0_columns)

        def passed_out(x, _):
            for c in range(3):
                end_out(c, x, w2p[c, x])
            return 0

        loop(passed_out, 0)

    @pl.when(jnp.logical_not(has[("tm", 1)]))
    def _():
        def last_out(x, _):
            w2 = chain_end(x)
            for c in range(3):
                end_out(c, x, w2[c])
            return 0

        loop(last_out, 0)

    for copies in (u_rows, u_columns, v1_copies, v2_copies, w1_copies, d_copy, *w_parts, w0_rows, w0_columns):
        sent(copies)


def per_device(sizes, provisional):
    block = jnp.swapaxes(provisional[0], 2, 3)
    _, _, X, Z, Y = block.shape
    f32 = jnp.float32
    padded = pltpu.VMEM((3, X + 2, Z, Y), f32)
    plain = pltpu.VMEM((3, X, Z, Y), f32)
    half = pltpu.VMEM((3, X // 2, Z, Y), f32)

    def edges(count):
        return [pltpu.VMEM((2, count, Z, LANES), f32)] * 2

    out = pl.pallas_call(
        functools.partial(kernel, *sizes),
        out_shape=jax.ShapeDtypeStruct(block.shape, f32),
        in_specs=[pl.BlockSpec(memory_space=pl.ANY)],
        out_specs=pl.BlockSpec(memory_space=pltpu.VMEM),
        scratch_shapes=[
            pltpu.VMEM((3, 3, X + 2, Z, Y), f32),
            *[padded] * 6,
            *[plain] * 7,
            *edges(4), *edges(2), *edges(1), *edges(1), *edges(1),
            *[half] * 4,
            pltpu.SemaphoreType.DMA,
            pltpu.SemaphoreType.DMA((5, 4)),
            pltpu.SemaphoreType.DMA((5, 4)),
            pltpu.SemaphoreType.DMA((X,)),
            pltpu.SemaphoreType.DMA((X,)),
        ],
        compiler_params=pltpu.CompilerParams(
            collective_id=0, has_side_effects=True, vmem_limit_bytes=40 * 1024 * 1024
        ),
    )(block)
    return jnp.swapaxes(out, 2, 3)[None]


def solution(mesh):
    sizes = tuple(mesh.shape[axis] for axis in ("tm", "gx", "gy"))
    spec = P("tm", None, None, None, "gx", "gy")
    return jax.shard_map(
        functools.partial(per_device, sizes), mesh=mesh, in_specs=(spec,), out_specs=spec,
        check_vma=False,
    )
```

```python
import functools

import jax
import jax.numpy as jnp
from jax import lax
from jax.experimental import pallas as pl
from jax.experimental.pallas import tpu as pltpu
from jax.sharding import PartitionSpec as P

viscosity = 0.1
slice_step = 0.25
half_step = 0.125
first_row = (5.0 / 24.0, 1.0 / 3.0, -1.0 / 24.0)
second_row = (-1.0 / 24.0, 1.0 / 3.0, 5.0 / 24.0)
q1 = tuple(slice_step * w for w in first_row)
q2 = tuple(slice_step * w for w in second_row)
LANES = 128


def kernel(
    n_tm, n_gx, n_gy, in_ref, out_ref,
    up, v1p, v2p, c0p, c1p, w0p, w1p, w2p, f0, s2, qa, qb, m1, m2,
    eu_s, eu_r, ev1_s, ev1_r, ev2_s, ev2_r, ew0_s, ew0_r, ew1_s, ew1_r,
    d_s, d_r, w_s, w_r,
    load_sem, send_sem, recv_sem, tm_send, tm_recv,
):
    _, _, X, Z, Y = in_ref.shape
    H = X // 2
    t, gx, gy = lax.axis_index("tm"), lax.axis_index("gx"), lax.axis_index("gy")
    has = {
        ("gx", 1): gx < n_gx - 1, ("gx", -1): gx > 0,
        ("gy", 1): gy < n_gy - 1, ("gy", -1): gy > 0,
        ("tm", 1): t < n_tm - 1, ("tm", -1): t > 0,
    }
    for axis in ("gx", "gy"):
        for step in (1, -1):
            for slice_ in (1, -1):
                has[(axis, step, slice_)] = jnp.logical_and(has[(axis, step)], has[("tm", slice_)])
    place = {"gx": gx, "gy": gy, "tm": t}

    def target(axis, step, slice_=0):
        size = {"gx": n_gx, "gy": n_gy, "tm": n_tm}
        moved = dict(place)
        moved[axis] = lax.rem(place[axis] + step + size[axis], size[axis])
        if slice_ != 0:
            moved["tm"] = lax.rem(t + slice_ + n_tm, n_tm)
        return (moved["tm"], moved["gx"], moved["gy"])

    load = pltpu.make_async_copy(in_ref, up.at[:, :, pl.ds(1, X)], load_sem)
    load.start()

    barrier = pltpu.get_barrier_semaphore()
    for peer, there in has.items():
        @pl.when(there)
        def _(peer=peer):
            pl.semaphore_signal(
                barrier, inc=1, device_id=target(*peer),
                device_id_type=pl.DeviceIdType.MESH,
            )
    peers = sum(jnp.where(there, 1, 0) for there in has.values())
    pl.semaphore_wait(barrier, peers)

    lane = lax.broadcasted_iota(jnp.int32, (Z, Y), 1)
    even = lane % 2 == 0
    elane = lax.broadcasted_iota(jnp.int32, (Z, LANES), 1)
    epair = elane // 2

    def remote(src, dst, p, d, axis, step, slice_=0):
        return pltpu.make_async_remote_copy(
            src_ref=src, dst_ref=dst, send_sem=send_sem.at[p, d], recv_sem=recv_sem.at[p, d],
            device_id=target(axis, step, slice_), device_id_type=pl.DeviceIdType.MESH,
        )

    def row(ref, i):
        return ref.at[:, :, pl.ds(i, 1)] if len(ref.shape) == 5 else ref.at[:, pl.ds(i, 1)]

    def rows_of(p, src, first, last, dst):
        return [
            (("gx", 1), remote(row(src, last), row(dst, 0), p, 0, "gx", 1)),
            (("gx", -1), remote(row(src, first), row(dst, X + 1), p, 1, "gx", -1)),
        ]

    def columns_of(p, es, er):
        return [
            (("gy", 1), remote(es.at[1], er.at[0], p, 2, "gy", 1)),
            (("gy", -1), remote(es.at[0], er.at[1], p, 3, "gy", -1)),
        ]

    def start(copies):
        for key, copy in copies:
            pl.when(has[key])(copy.start)

    def arrive(copies):
        for (axis, *steps), copy in copies:
            pl.when(has[(axis, *[-step for step in steps])])(copy.wait_recv)

    def sent(copies):
        for key, copy in copies:
            pl.when(has[key])(copy.wait_send)

    def no_rows(dst):
        for key, i in ((("gx", -1), 0), (("gx", 1), X + 1)):
            @pl.when(jnp.logical_not(has[key]))
            def _(i=i):
                where_ = row(dst, i)
                where_[...] = jnp.zeros(where_.shape, jnp.float32)

    def no_columns(er):
        for key, i in ((("gy", -1), 0), (("gy", 1), 1)):
            @pl.when(jnp.logical_not(has[key]))
            def _(i=i):
                er[i] = jnp.zeros(er.shape[1:], jnp.float32)

    def G(get, x, low, high, k):
        mid = [get(c, x + 1) for c in range(3)]
        a = [0.5 * mid[0], (0.5 / k) * mid[1], 0.5 * mid[2]]
        nu = [viscosity, viscosity / (k * k), viscosity]
        ahead = [nu[i] - a[i] for i in range(3)]
        behind = [nu[i] + a[i] for i in range(3)]
        result = []
        for c in range(3):
            u = mid[c]
            at = c * X + x
            if k == 1:
                h = pltpu.roll(high, LANES - 1 - at, 1)
                l = pltpu.roll(low, lax.rem(LANES - at, LANES), 1)
            else:
                h = pltpu.roll(high, LANES - 2 - 2 * at, 1)
                l = pltpu.roll(low, lax.rem(LANES - 2 * at, LANES), 1)
            wide = Y // LANES
            north = jnp.where(lane >= Y - k, jnp.concatenate([h] * wide, 1), pltpu.roll(u, Y - k, 1))
            south = jnp.where(lane < k, jnp.concatenate([l] * wide, 1), pltpu.roll(u, k, 1))
            result.append(
                (ahead[0] * get(c, x + 2) + behind[0] * get(c, x))
                + (ahead[1] * north + behind[1] * south)
                + (ahead[2] * pltpu.roll(u, Z - 1, 0) + behind[2] * pltpu.roll(u, 1, 0))
                - (2.0 * sum(nu)) * u
            )
        return result

    def R(u):
        return 0.5 * (u + jnp.where(even, pltpu.roll(u, Y - 1, 1), pltpu.roll(u, 1, 1)))

    def put(acc, column, at, k):
        return jnp.where((elane if k == 1 else epair) == at, column, acc)

    def put_both(pair, u, at, k):
        return (put(pair[0], u[:, :1], at, k), put(pair[1], u[:, Y - 1:], at, k))

    blank = jnp.zeros((Z, LANES), jnp.float32)
    blanks = (blank, blank)

    def loop(body, carry, count=X, first=0):
        return lax.fori_loop(first, count, body, carry, unroll=2 if (count - first) % 2 == 0 else 1)

    def edges_first(body, carry, copies):
        carry = loop(lambda i, carry: body(i * (X - 1), carry), carry, 2)
        start(copies)
        return loop(body, carry, X - 1, 1)

    u_rows = rows_of(0, in_ref, 0, X - 1, up)
    start(u_rows)
    no_rows(up)
    no_columns(eu_r)
    load.wait()

    def pack_u(x, carry):
        nodes, coarse = list(carry[:3]), carry[3]
        for c in range(3):
            at = c * X + x
            for n in range(3):
                nodes[n] = put_both(nodes[n], up[n, c, x + 1], at, 1)
            coarse = put_both(coarse, R(up[0, c, x + 1]), at, 2)
        return (*nodes, coarse)

    packed = loop(pack_u, (blanks,) * 4)
    for n in range(4):
        for side in range(2):
            eu_s[side, n] = packed[n][side]
    u_columns = columns_of(0, eu_s, eu_r)
    start(u_columns)
    arrive(u_rows)
    arrive(u_columns)

    def sweep_first(x, carry):
        fine, coarse = carry
        fluxes = [
            G(lambda c, i, n=n: up[n, c, i], x, eu_r[0, n], eu_r[1, n], 1) for n in range(3)
        ]
        for c in range(3):
            a, b, d = (fluxes[n][c] for n in range(3))
            v1 = up[0, c, x + 1] + (q1[0] * a + q1[1] * b + q1[2] * d)
            v1p[c, x + 1] = v1
            f0[c, x] = a
            s2[c, x] = q2[0] * a + (q2[1] - half_step) * b + q2[2] * d
            at = c * X + x
            fine = put_both(fine, v1, at, 1)
            coarse = put_both(coarse, R(v1), at, 2)
        return fine, coarse

    v1_rows = rows_of(1, v1p, 1, X, v1p)
    v1_columns = columns_of(1, ev1_s, ev1_r)
    v1_copies = v1_rows + v1_columns
    fine, coarse = edges_first(sweep_first, (blanks, blanks), v1_rows)
    for side in range(2):
        ev1_s[side, 0] = fine[side]
        ev1_s[side, 1] = coarse[side]
    start(v1_columns)
    no_rows(v1p)
    no_columns(ev1_r)

    def restrict_start(i, _):
        for c in range(3):
            c0p[c, i] = R(up[0, c, i])
        return 0

    loop(restrict_start, 0, X + 2)

    @pl.when(has[("tm", -1)])
    def _():
        def base_start(x, _):
            b0 = G(lambda c, i: c0p[c, i], x, eu_r[0, 3], eu_r[1, 3], 2)
            for c in range(3):
                m1[c, x] = -half_step * b0[c]
            return 0

        loop(base_start, 0)

    arrive(v1_copies)

    def sweep_second(x, fine):
        h1 = G(lambda c, i: v1p[c, i], x, ev1_r[0, 0], ev1_r[1, 0], 1)
        for c in range(3):
            v2 = v1p[c, x + 1] + half_step * h1[c] + s2[c, x]
            v2p[c, x + 1] = v2
            a = f0[c, x]
            qa[c, x] = q1[0] * a + q1[1] * h1[c]
            qb[c, x] = q2[0] * a + q2[1] * h1[c]
            fine = put_both(fine, v2, c * X + x, 1)
        return fine

    v2_rows = rows_of(2, v2p, 1, X, v2p)
    v2_columns = columns_of(2, ev2_s, ev2_r)
    v2_copies = v2_rows + v2_columns
    fine = edges_first(sweep_second, blanks, v2_rows)
    for side in range(2):
        ev2_s[side, 0] = fine[side]
    start(v2_columns)
    no_rows(v2p)
    no_columns(ev2_r)

    def detail(x, _):
        for c in range(3):
            a, b = v2p[c, x + 1], v2p[c, x + H + 1]
            d_s[c, x] = jnp.where(even, a - R(a), b - R(b))
        return 0

    def along(src, dst, p):
        return pltpu.make_async_remote_copy(
            src_ref=src, dst_ref=dst, send_sem=tm_send.at[p], recv_sem=tm_recv.at[p],
            device_id=target("tm", 1), device_id_type=pl.DeviceIdType.MESH,
        )

    d_copy = [(("tm", 1), along(d_s, d_r, 0))]
    spans = [(0, 1), (H - 1, 1)]
    spans += [(i, min(2, H - 1 - i)) for i in range(1, H - 1, 2)]
    spans = spans[: max(1, H)]
    w_parts = [
        [(("tm", 1), along(w_s.at[:, pl.ds(i, n)], w_r.at[:, pl.ds(i, n)], 1 + j))]
        for j, (i, n) in enumerate(spans)
    ]
    w0_rows = [
        (("gx", 1, 1), remote(row(w2p, X - 1), row(w0p, 0), 3, 0, "gx", 1, 1)),
        (("gx", -1, 1), remote(row(w2p, 0), row(w0p, X + 1), 3, 1, "gx", -1, 1)),
    ]
    w0_columns = [
        (("gy", 1, 1), remote(ew0_s.at[1], ew0_r.at[0], 3, 2, "gy", 1, 1)),
        (("gy", -1, 1), remote(ew0_s.at[0], ew0_r.at[1], 3, 3, "gy", -1, 1)),
    ]

    @pl.when(has[("tm", 1)])
    def _():
        loop(detail, 0, H)

    start(d_copy)

    def restrict_middle(i, _):
        for c in range(3):
            c1p[c, i] = R(v1p[c, i])
        return 0

    loop(restrict_middle, 0, X + 2)

    def base_middle(x, _):
        b1 = G(lambda c, i: c1p[c, i], x, ev1_r[0, 1], ev1_r[1, 1], 2)
        for c in range(3):
            m2[c, x] = -half_step * b1[c]
        return 0

    loop(base_middle, 0)
    arrive(v2_copies)

    leader = t == 0

    def sweep_third(x, coarse):
        h2 = G(lambda c, i: v2p[c, i], x, ev2_r[0, 0], ev2_r[1, 0], 1)
        for c in range(3):
            a1 = R(qa[c, x] + q1[2] * h2[c])
            a2 = R(qb[c, x] + q2[2] * h2[c])
            m2[c, x] = m2[c, x] + a2
            if coarse is None:
                m1[c, x] = m1[c, x] + a1
            else:
                w1 = c0p[c, x + 1] + a1
                w1p[c, x + 1] = w1
                coarse = put_both(coarse, w1, c * X + x, 2)
        return coarse

    w1_rows = rows_of(4, w1p, 1, X, w1p)
    w1_columns = columns_of(4, ew1_s, ew1_r)
    w1_copies = w1_rows + w1_columns

    @pl.when(leader)
    def _():
        coarse = edges_first(sweep_third, blanks, w1_rows)
        for side in range(2):
            ew1_s[side, 0] = coarse[side]

    @pl.when(has[("tm", -1)])
    def _():
        loop(lambda x, _: sweep_third(x, None) or 0, 0)
        no_rows(w0p)
        no_columns(ew0_r)

        def unpack(x, _):
            for c in range(3):
                w = w_r[c, x]
                w0p[c, x + 1] = jnp.where(even, w, pltpu.roll(w, 1, 1))
                w0p[c, x + H + 1] = jnp.where(even, pltpu.roll(w, Y - 1, 1), w)
            return 0

        for part, (i, n) in zip(w_parts, spans):
            arrive(part)
            loop(unpack, 0, i + n, i)
        arrive(w0_rows)
        arrive(w0_columns)

        def chain_middle(x, coarse):
            g = G(lambda c, i: w0p[c, i], x, ew0_r[0, 0], ew0_r[1, 0], 2)
            for c in range(3):
                w1 = w0p[c, x + 1] + half_step * g[c] + m1[c, x]
                w1p[c, x + 1] = w1
                coarse = put_both(coarse, w1, c * X + x, 2)
            return coarse

        coarse = edges_first(chain_middle, blanks, w1_rows)
        for side in range(2):
            ew1_s[side, 0] = coarse[side]

    start(w1_columns)
    no_rows(w1p)
    no_columns(ew1_r)

    def middle_out(x, _):
        for c in range(3):
            out_ref[1, c, x] = v1p[c, x + 1] + (w1p[c, x + 1] - c1p[c, x + 1])
        return 0

    loop(middle_out, 0)

    @pl.when(leader)
    def _():
        def start_out(x, _):
            for c in range(3):
                out_ref[0, c, x] = up[0, c, x + 1]
            return 0

        loop(start_out, 0)

    @pl.when(has[("tm", -1)])
    def _():
        arrive(d_copy)

        def start_out(x, _):
            for c in range(3):
                d = d_r[c, x]
                a = jnp.where(even, d, -pltpu.roll(d, 1, 1))
                b = jnp.where(even, -pltpu.roll(d, Y - 1, 1), d)
                out_ref[0, c, x] = w0p[c, x + 1] + a
                out_ref[0, c, x + H] = w0p[c, x + H + 1] + b
            return 0

        loop(start_out, 0, H)

    arrive(w1_copies)

    def chain_end(x):
        g = G(lambda c, i: w1p[c, i], x, ew1_r[0, 0], ew1_r[1, 0], 2)
        return [w1p[c, x + 1] + half_step * g[c] + m2[c, x] for c in range(3)]

    def end_out(c, x, w2):
        v2 = v2p[c, x + 1]
        out_ref[2, c, x] = v2 + (w2 - R(v2))

    @pl.when(has[("tm", 1)])
    def _():
        def pair(x, coarse):
            ends = (chain_end(x), chain_end(x + H))
            for c in range(3):
                w_s[c, x] = jnp.where(even, ends[0][c], ends[1][c])
                for end, i in zip(ends, (x, x + H)):
                    w2p[c, i] = end[c]
                    coarse = put_both(coarse, end[c], c * X + i, 2)
            return coarse

        coarse = blanks
        for j, (part, (i, n)) in enumerate(zip(w_parts, spans)):
            coarse = loop(pair, coarse, i + n, i)
            start(part)
            if j == min(1, len(spans) - 1):
                start(w0_rows)
        for side in range(2):
            ew0_s[side, 0] = coarse[side]
        start(w0_columns)

        def passed_out(x, _):
            for c in range(3):
                end_out(c, x, w2p[c, x])
            return 0

        loop(passed_out, 0)

    @pl.when(jnp.logical_not(has[("tm", 1)]))
    def _():
        def last_out(x, _):
            w2 = chain_end(x)
            for c in range(3):
                end_out(c, x, w2[c])
            return 0

        loop(last_out, 0)

    for copies in (u_rows, u_columns, v1_copies, v2_copies, w1_copies, d_copy, *w_parts, w0_rows, w0_columns):
        sent(copies)


def per_device(sizes, provisional):
    block = jnp.swapaxes(provisional[0], 2, 3)
    _, _, X, Z, Y = block.shape
    f32 = jnp.float32
    padded = pltpu.VMEM((3, X + 2, Z, Y), f32)
    plain = pltpu.VMEM((3, X, Z, Y), f32)
    half = pltpu.VMEM((3, X // 2, Z, Y), f32)

    def edges(count):
        return [pltpu.VMEM((2, count, Z, LANES), f32)] * 2

    out = pl.pallas_call(
        functools.partial(kernel, *sizes),
        out_shape=jax.ShapeDtypeStruct(block.shape, f32),
        in_specs=[pl.BlockSpec(memory_space=pl.ANY)],
        out_specs=pl.BlockSpec(memory_space=pltpu.VMEM),
        scratch_shapes=[
            pltpu.VMEM((3, 3, X + 2, Z, Y), f32),
            *[padded] * 6,
            *[plain] * 7,
            *edges(4), *edges(2), *edges(1), *edges(1), *edges(1),
            *[half] * 4,
            pltpu.SemaphoreType.DMA,
            pltpu.SemaphoreType.DMA((5, 4)),
            pltpu.SemaphoreType.DMA((5, 4)),
            pltpu.SemaphoreType.DMA((X,)),
            pltpu.SemaphoreType.DMA((X,)),
        ],
        compiler_params=pltpu.CompilerParams(
            collective_id=0, has_side_effects=True, vmem_limit_bytes=40 * 1024 * 1024
        ),
    )(block)
    return jnp.swapaxes(out, 2, 3)[None]


def solution(mesh):
    sizes = tuple(mesh.shape[axis] for axis in ("tm", "gx", "gy"))
    spec = P("tm", None, None, None, "gx", "gy")
    return jax.shard_map(
        functools.partial(per_device, sizes), mesh=mesh, in_specs=(spec,), out_specs=spec,
        check_vma=False,
    )
```
